32 devices in a mesh: groups: 2 (over y), ty: 4 (over z), tx: 2 (over x), pz: 2 (over core).
Axes of the slice: x: 2, y: 2, z: 4, core: 2. Of those that a mesh axis runs over, the one named last changes fastest.
Arguments:
- object_field: float32 [2, 2048, 512], P(None, ('groups', 'ty'), 'tx'), parts along dimension 1, may hold values from -6 to 6
- probe_wave: float32 [2, 256, 256], replicated, may hold values from -6 to 6
- amplitudes: float32 [192, 256, 256], P(('groups', 'ty', 'tx', 'pz')), parts along dimension 0, may hold values from 0.3 to 3
- positions: int32 [192, 2], P(('groups', 'ty', 'tx', 'pz')), parts along dimension 0, may hold values from 0 to 1023, as said below
- counts: int32 [32], P(('groups', 'ty', 'tx', 'pz')), parts along dimension 0, may hold values from 1 to 6, as said below
Outputs:
- object_grad: float32 [2, 2048, 512], P(None, ('groups', 'ty'), 'tx'), parts along dimension 1
- probe_grad: float32 [4, 256, 256], P('groups'), parts along dimension 0
The draws below stay inside these ranges and needn't reach their ends.
There are 2 independent parts, one for each index of `groups`. The reference program is written for one: setup_inputs(seed, part) draws one part's arguments, and reference() takes and returns one part's arrays. A program takes and returns all parts, laid end to end along the dimension named above; an argument that names none is the same for every part. Nothing has to cross between parts.
Inputs may be any that keep to these rules, and one draw needn't show every extreme that they name: `positions`: the slots of owner d are rows d * 6 to d * 6 + 5. With owner d = (a * 2 + b) * 2 + c, every slot's row offset lies in a * 256 to a * 256 + 255 and its column offset in b * 256 to b * 256 + 255. `counts`: some owner uses all 6 slots in every draw.
All inputs are finite; a program needn't handle non-finite values.
Results may differ from the reference program's by a relative error of at most 0.0003.
Values sent between devices are 32-bit elements; how exact they have to be, the bound alone decides.
A program may use at most 64 MiB of HBM per device.

```python
import math
import jax
import jax.numpy as jnp
from jax import lax

PROBE = 256
TH = 256
TW = 256
CAP = 6
NY = 1024
NX = 512
NDEV = 16
NPOS = 96


def draw_positions(key, part):
    key = jax.random.fold_in(key, 11)
    tiles_x = NX // TW
    per_tile = NDEV // (NY // TH * tiles_x)
    owner_dev = jnp.arange(NPOS, dtype=jnp.int32) // CAP
    tile_row = owner_dev // (tiles_x * per_tile)
    tile_col = owner_dev // per_tile % tiles_x
    key_rows, key_cols = jax.random.split(key)
    row_offsets = tile_row * TH + jax.random.randint(key_rows, (NPOS,), 0, TH, dtype=jnp.int32)
    col_offsets = tile_col * TW + jax.random.randint(key_cols, (NPOS,), 0, TW, dtype=jnp.int32)
    row_offsets = row_offsets.at[0].set(0).at[NPOS - CAP].set(NY - 1)
    col_offsets = col_offsets.at[0].set(0).at[NPOS - CAP].set(NX - 1)
    return jnp.stack([row_offsets, col_offsets], axis=1).astype(jnp.int32)


def draw_counts(key, part):
    key = jax.random.fold_in(key, 23)
    key_heavy, key_light, key_chosen = jax.random.split(key, 3)
    heavy_pick = jax.random.randint(key_heavy, (NDEV,), 0, 4, dtype=jnp.int32) == 0
    light_load = jax.random.randint(key_light, (NDEV,), 1, CAP // 3 + 1, dtype=jnp.int32)
    loads = jnp.where(heavy_pick, CAP, light_load)
    chosen = jax.random.randint(key_chosen, (), 0, NDEV, dtype=jnp.int32)
    return loads.at[chosen].set(CAP).astype(jnp.int32)


def block_scale(key, shape, cuts, least, top_value):
    factor_of = 1.0
    for dim, shards_of in cuts:
        heights = jax.random.uniform(jax.random.fold_in(jax.random.fold_in(key, 6), dim), (shards_of,), jnp.float32, least / len(cuts), top_value / len(cuts))
        factor_of = factor_of * jnp.repeat(jnp.exp(heights), shape[dim] // shards_of).reshape((-1,) + (1,) * (len(shape) - 1 - dim))
    return factor_of


def normal_values(own_key, shape, scale, reach, shards=(), kind=jnp.bfloat16):
    loudness = block_scale(own_key, shape, shards, -0.22, 0.18) if shards else 1.0
    entries = jax.random.normal(own_key, shape, jnp.float32) * scale * loudness
    return jnp.minimum(jnp.maximum(entries, -reach), reach).astype(kind)


def setup_inputs(seed: int = 0, part: int = 0) -> dict:
    streams_of = jax.random.split(jax.random.key(seed), 6)
    own_keys = jax.random.split(jax.random.fold_in(streams_of[5], part), 6)
    object_field = normal_values(own_keys[0], (2, NY, NX), 1.0, 6.0, ((1, 4), (2, 2)), jnp.float32)
    probe_wave = normal_values(streams_of[1], (2, PROBE, PROBE), 1.0, 6.0, (), jnp.float32)
    amplitudes = jnp.clip(jnp.exp(math.log(3.0) - 2.3025851 * jax.random.uniform(own_keys[2], (NPOS, PROBE, PROBE), jnp.float32) ** block_scale(own_keys[2], (NPOS, PROBE, PROBE), ((0, 16),), -0.2, 0.2)), 0.3, 3.0)
    positions = draw_positions(jax.random.fold_in(jax.random.fold_in(streams_of[5], part), 71), part)
    counts = draw_counts(jax.random.fold_in(jax.random.fold_in(streams_of[5], part), 71), part)
    return {"object_field": object_field, "probe_wave": probe_wave, "amplitudes": amplitudes, "positions": positions, "counts": counts}


def dft_tables(probe_size):
    ladder = jnp.arange(probe_size, dtype=jnp.int32)
    product = ladder[:, None] * ladder[None, :] % probe_size
    phase = product.astype(jnp.float32) * (2.0 * math.pi / probe_size)
    factor = 1.0 / math.sqrt(probe_size)
    return (jnp.cos(phase) * factor, -jnp.sin(phase) * factor)

def matmul(left, right):
    return jnp.dot(left, right, precision=lax.Precision.HIGHEST, preferred_element_type=jnp.float32)

def transform(real_part, imag_part, cos_tab, sin_tab):
    mid_re = matmul(cos_tab, real_part) - matmul(sin_tab, imag_part)
    mid_im = matmul(cos_tab, imag_part) + matmul(sin_tab, real_part)
    out_re = matmul(mid_re, cos_tab) - matmul(mid_im, sin_tab)
    out_im = matmul(mid_re, sin_tab) + matmul(mid_im, cos_tab)
    return (out_re, out_im)

def slot_grad(patch_view, probe_wave, amplitude, valid_mask, cos_tab, sin_tab):
    probe_re, probe_im = (probe_wave[0], probe_wave[1])
    patch_re, patch_im = (patch_view[0], patch_view[1])
    exit_re = probe_re * patch_re - probe_im * patch_im
    exit_im = probe_re * patch_im + probe_im * patch_re
    far_re, far_im = transform(exit_re, exit_im, cos_tab, sin_tab)
    magnitude = jnp.sqrt(far_re * far_re + far_im * far_im + 0.01)
    resid_re = valid_mask * (far_re - amplitude * far_re / magnitude)
    resid_im = valid_mask * (far_im - amplitude * far_im / magnitude)
    back_re, back_im = transform(resid_re, resid_im, cos_tab, -sin_tab)
    patch_grad = jnp.stack([probe_re * back_re + probe_im * back_im, probe_re * back_im - probe_im * back_re])
    probe_term = jnp.stack([patch_re * back_re + patch_im * back_im, patch_re * back_im - patch_im * back_re])
    return (patch_grad, probe_term)

def reference(object_field, probe_wave, amplitudes, positions, counts):
    probe_size = PROBE
    cos_tab, sin_tab = dft_tables(probe_size)
    padded = jnp.concatenate([object_field, object_field[:, :probe_size, :]], axis=1)
    padded = jnp.concatenate([padded, padded[:, :, :probe_size]], axis=2)
    zero_index = jnp.zeros((), jnp.int32)

    def visit_slot(loop_state, scan_item):
        grad_buffer, probe_acc = loop_state
        position, amplitude, flat_index = scan_item
        valid_mask = (flat_index % CAP < counts[flat_index // CAP]).astype(jnp.float32)
        corner = (zero_index, position[0].astype(jnp.int32), position[1].astype(jnp.int32))
        patch_view = lax.dynamic_slice(padded, corner, (2, probe_size, probe_size))
        patch_grad, probe_term = slot_grad(patch_view, probe_wave, amplitude, valid_mask, cos_tab, sin_tab)
        current = lax.dynamic_slice(grad_buffer, corner, (2, probe_size, probe_size))
        grad_buffer = lax.dynamic_update_slice(grad_buffer, current + patch_grad, corner)
        return ((grad_buffer, probe_acc + probe_term), None)
    start_buffer = jnp.zeros((2, NY + probe_size, NX + probe_size), jnp.float32)
    start_probe = jnp.zeros((2, probe_size, probe_size), jnp.float32)
    slot_ids = jnp.arange(NPOS, dtype=jnp.int32)
    (grad_buffer, probe_grad), _ = lax.scan(visit_slot, (start_buffer, start_probe), (positions, amplitudes, slot_ids))
    object_grad = grad_buffer[:, :NY, :NX]
    object_grad = object_grad.at[:, :probe_size, :].add(grad_buffer[:, NY:, :NX])
    object_grad = object_grad.at[:, :, :probe_size].add(grad_buffer[:, :NY, NX:])
    object_grad = object_grad.at[:, :probe_size, :probe_size].add(grad_buffer[:, NY:, NX:])
    return (object_grad, probe_grad)
```

```python
import functools

import jax
import jax.numpy as jnp
import numpy as np
from jax import lax
from jax.experimental import pallas as pl
from jax.experimental.pallas import tpu as pltpu
from jax.sharding import PartitionSpec as P


def passed_along(value, axis, by):
    peers = lax.axis_size(axis)
    return lax.ppermute(value, axis, [(i, (i + by) % peers) for i in range(peers)])


def half_tables(size):
    half = size // 2
    pixel = np.arange(half)
    tables = []
    for parity in (0, 1):
        freq = 2 * np.arange(half) + parity
        phase = (freq[:, None] * pixel[None, :] % size) * (2.0 * np.pi / size)
        cos_tab = np.cos(phase) / np.sqrt(size)
        sin_tab = np.sin(phase) / np.sqrt(size)
        full = np.block([[cos_tab, sin_tab], [-sin_tab, cos_tab]])
        tables += [full, full.T]
    full = np.stack(tables)
    high = full.astype(jnp.bfloat16)
    low = (full - high.astype(np.float64)).astype(jnp.bfloat16)
    return np.stack([high, low], axis=1)


def order_table(size):
    order = np.concatenate([np.arange(0, size, 2), np.arange(1, size, 2)])
    table = np.zeros((size, size), np.float32)
    table[order, np.arange(size)] = 1.0
    return table.astype(jnp.bfloat16)


def split(value):
    high = value.astype(jnp.bfloat16)
    low = (value - high.astype(jnp.float32)).astype(jnp.bfloat16)
    return high, low


def mm(left, right):
    return jnp.dot(left, right, preferred_element_type=jnp.float32)


def left_product(tab_ref, which, value):
    high, low = split(value)
    return mm(tab_ref[which, 0], high) + mm(tab_ref[which, 0], low) + mm(tab_ref[which, 1], high)


def right_product(tab_ref, which, value):
    high, low = split(value)
    return mm(high, tab_ref[which, 0]) + mm(low, tab_ref[which, 0]) + mm(high, tab_ref[which, 1])


def forward(re, im, tab_ref):
    half = re.shape[0] // 2
    cat = jnp.concatenate
    even = cat([re[:half] + re[half:], im[:half] + im[half:]], 0)
    odd = cat([re[:half] - re[half:], im[:half] - im[half:]], 0)
    even = left_product(tab_ref, 0, even)
    odd = left_product(tab_ref, 2, odd)
    re = cat([even[:half], odd[:half]], 0)
    im = cat([even[half:], odd[half:]], 0)
    even = cat([re[:, :half] + re[:, half:], im[:, :half] + im[:, half:]], 1)
    odd = cat([re[:, :half] - re[:, half:], im[:, :half] - im[:, half:]], 1)
    even = right_product(tab_ref, 1, even)
    odd = right_product(tab_ref, 3, odd)
    return cat([even[:, :half], odd[:, :half]], 1), cat([even[:, half:], odd[:, half:]], 1)


def backward(re, im, tab_ref):
    half = re.shape[0] // 2
    cat = jnp.concatenate
    even = right_product(tab_ref, 0, cat([re[:, :half], im[:, :half]], 1))
    odd = right_product(tab_ref, 2, cat([re[:, half:], im[:, half:]], 1))
    total, diff = even + odd, even - odd
    re = cat([total[:, :half], diff[:, :half]], 1)
    im = cat([total[:, half:], diff[:, half:]], 1)
    even = left_product(tab_ref, 1, cat([re[:half], im[:half]], 0))
    odd = left_product(tab_ref, 3, cat([re[half:], im[half:]], 0))
    total, diff = even + odd, even - odd
    return cat([total[:half], diff[:half]], 0), cat([total[half:], diff[half:]], 0)


def rolled(value, rows, cols):
    return pltpu.roll(pltpu.roll(value, rows, 0), cols, 1)


def compute_kernel(
    pos_ref, cnt_ref, own_ref, right_ref, down_ref, diag_ref, probe_ref, amp_ref, tab_ref, ord_ref,
    grad_ref, pgrad_ref, held_ref, ampl_ref, sem_ref,
):
    slots, size = amp_ref.shape[0], amp_ref.shape[1]
    amp_copies = [
        pltpu.make_async_copy(
            amp_ref.at[:, :, pl.ds(part * 128, 128)], ampl_ref.at[part], sem_ref.at[part]
        )
        for part in range(size // 128)
    ]
    for copy in amp_copies:
        copy.start()
    row_base = lax.axis_index("ty") * size
    col_base = lax.axis_index("tx") * size
    used_count = cnt_ref[0]
    half = size // 2
    row_id = lax.broadcasted_iota(jnp.int32, (size, size), 0)
    col_id = lax.broadcasted_iota(jnp.int32, (size, size), 1)
    pgrad_ref[...] = jnp.zeros_like(pgrad_ref)
    for copy in amp_copies:
        copy.wait()

    def visit(slot, carry):
        row = pos_ref[slot, 0] - row_base
        col = pos_ref[slot, 1] - col_base
        used = (slot < used_count).astype(jnp.float32)
        above = row_id < row
        before = col_id < col
        patch = [
            jnp.where(
                above,
                jnp.where(before, diag_ref[p], down_ref[p]),
                jnp.where(before, right_ref[p], own_ref[p]),
            )
            for p in range(2)
        ]
        probe = [rolled(probe_ref[p], row, col) for p in range(2)]
        exit_re = probe[0] * patch[0] - probe[1] * patch[1]
        exit_im = probe[0] * patch[1] + probe[1] * patch[0]
        far_re, far_im = forward(exit_re, exit_im, tab_ref)
        amp = jnp.concatenate(
            [
                jnp.concatenate(
                    [ampl_ref[part, slot, pl.ds(parity, half, 2), :] for part in range(size // 128)], 1
                )
                for parity in (0, 1)
            ],
            0,
        )
        high, low = split(amp)
        amp = mm(high, ord_ref[...]) + mm(low, ord_ref[...])
        gain = used * (1.0 - amp * lax.rsqrt(far_re * far_re + far_im * far_im + 0.01))
        back_re, back_im = backward(far_re * gain, far_im * gain, tab_ref)
        held_ref[slot, 0] = probe[0] * back_re + probe[1] * back_im
        held_ref[slot, 1] = probe[0] * back_im - probe[1] * back_re
        up, left = (size - row) % size, (size - col) % size
        pgrad_ref[0] += rolled(patch[0] * back_re + patch[1] * back_im, up, left)
        pgrad_ref[1] += rolled(patch[0] * back_im - patch[1] * back_re, up, left)
        return carry

    lax.fori_loop(0, slots, visit, 0)

    chunk = 16

    def gather(step, carry):
        base = pl.multiple_of(step * chunk, chunk)
        row_part = base + lax.broadcasted_iota(jnp.int32, (chunk, size), 0)
        col_part = lax.broadcasted_iota(jnp.int32, (chunk, size), 1)
        for p in range(2):
            sums = [jnp.zeros((chunk, size), jnp.float32) for _ in range(4)]
            for slot in range(slots):
                above = row_part < pos_ref[slot, 0] - row_base
                before = col_part < pos_ref[slot, 1] - col_base
                part = held_ref[slot, p, pl.ds(base, chunk), :]
                low = jnp.where(above, part, 0.0)
                top = part - low
                low_left = jnp.where(before, low, 0.0)
                top_left = jnp.where(before, top, 0.0)
                sums = [
                    sums[0] + (top - top_left),
                    sums[1] + top_left,
                    sums[2] + (low - low_left),
                    sums[3] + low_left,
                ]
            for quad in range(4):
                grad_ref[quad, p, pl.ds(base, chunk), :] = sums[quad]
        return carry

    lax.fori_loop(0, size // chunk, gather, 0)


def per_device(object_field, probe_wave, amplitudes, positions, counts):
    size = probe_wave.shape[1]
    slots = positions.shape[0]
    right = passed_along(object_field, "tx", -1)
    down = passed_along(object_field, "ty", -1)
    diag = passed_along(right, "ty", -1)
    vmem = pl.BlockSpec(memory_space=pltpu.VMEM)
    smem = pl.BlockSpec(memory_space=pltpu.SMEM)
    grads, probe_part = pl.pallas_call(
        compute_kernel,
        out_shape=(
            jax.ShapeDtypeStruct((4, 2, size, size), jnp.float32),
            jax.ShapeDtypeStruct((2, size, size), jnp.float32),
        ),
        in_specs=[smem, smem] + [vmem] * 5 + [pl.BlockSpec(memory_space=pl.ANY)] + [vmem] * 2,
        out_specs=(vmem, vmem),
        scratch_shapes=[
            pltpu.VMEM((slots, 2, size, size), jnp.float32),
            pltpu.VMEM((size // 128, slots, size, 128), jnp.float32),
            pltpu.SemaphoreType.DMA((size // 128,)),
        ],
        compiler_params=pltpu.CompilerParams(vmem_limit_bytes=48 * 1024 * 1024),
    )(
        positions, counts, object_field, right, down, diag, probe_wave, amplitudes,
        jnp.asarray(half_tables(size)), jnp.asarray(order_table(size)),
    )
    probe_grad = lax.psum(probe_part, ("ty", "tx", "pz"))
    from_right = passed_along(jnp.stack([grads[1], grads[3]]), "tx", 1)
    from_down = passed_along(grads[2] + from_right[1], "ty", 1)
    object_grad = lax.psum(grads[0] + from_right[0] + from_down, "pz")
    return object_grad, probe_grad


def solution(mesh):
    return jax.shard_map(
        per_device,
        mesh=mesh,
        in_specs=(
            P(None, ("groups", "ty"), "tx"),
            P(),
            P(("groups", "ty", "tx", "pz"), None, None),
            P(("groups", "ty", "tx", "pz"), None),
            P(("groups", "ty", "tx", "pz")),
        ),
        out_specs=(P(None, ("groups", "ty"), "tx"), P("groups", None, None)),
        check_vma=False,
    )
```

```python
import jax
import jax.numpy as jnp
import numpy as np
from jax import lax
from jax.experimental import pallas as pl
from jax.experimental.pallas import tpu as pltpu
from jax.sharding import PartitionSpec as P


def half_tables(size):
    half = size // 2
    pixel = np.arange(half)
    tables = []
    for parity in (0, 1):
        freq = 2 * np.arange(half) + parity
        phase = (freq[:, None] * pixel[None, :] % size) * (2.0 * np.pi / size)
        cos_tab = np.cos(phase) / np.sqrt(size)
        sin_tab = np.sin(phase) / np.sqrt(size)
        full = np.block([[cos_tab, sin_tab], [-sin_tab, cos_tab]])
        tables += [full, full.T]
    full = np.stack(tables)
    high = full.astype(jnp.bfloat16)
    low = (full - high.astype(np.float64)).astype(jnp.bfloat16)
    return np.stack([high, low], axis=1)


def order_table(size):
    order = np.concatenate([np.arange(0, size, 2), np.arange(1, size, 2)])
    table = np.zeros((size, size), np.float32)
    table[order, np.arange(size)] = 1.0
    return table.astype(jnp.bfloat16)


def split(value):
    high = value.astype(jnp.bfloat16)
    low = (value - high.astype(jnp.float32)).astype(jnp.bfloat16)
    return high, low


def mm(left, right):
    return jnp.dot(left, right, preferred_element_type=jnp.float32)


def left_product(tab_ref, which, value):
    high, low = split(value)
    return mm(tab_ref[which, 0], high) + mm(tab_ref[which, 0], low) + mm(tab_ref[which, 1], high)


def right_product(tab_ref, which, value):
    high, low = split(value)
    return mm(high, tab_ref[which, 0]) + mm(low, tab_ref[which, 0]) + mm(high, tab_ref[which, 1])


def forward(re, im, tab_ref):
    half = re.shape[0] // 2
    cat = jnp.concatenate
    even = cat([re[:half] + re[half:], im[:half] + im[half:]], 0)
    odd = cat([re[:half] - re[half:], im[:half] - im[half:]], 0)
    even = left_product(tab_ref, 0, even)
    odd = left_product(tab_ref, 2, odd)
    re = cat([even[:half], odd[:half]], 0)
    im = cat([even[half:], odd[half:]], 0)
    even = cat([re[:, :half] + re[:, half:], im[:, :half] + im[:, half:]], 1)
    odd = cat([re[:, :half] - re[:, half:], im[:, :half] - im[:, half:]], 1)
    even = right_product(tab_ref, 1, even)
    odd = right_product(tab_ref, 3, odd)
    return cat([even[:, :half], odd[:, :half]], 1), cat([even[:, half:], odd[:, half:]], 1)


def backward(re, im, tab_ref):
    half = re.shape[0] // 2
    cat = jnp.concatenate
    even = right_product(tab_ref, 0, cat([re[:, :half], im[:, :half]], 1))
    odd = right_product(tab_ref, 2, cat([re[:, half:], im[:, half:]], 1))
    total, diff = even + odd, even - odd
    re = cat([total[:, :half], diff[:, :half]], 1)
    im = cat([total[:, half:], diff[:, half:]], 1)
    even = left_product(tab_ref, 1, cat([re[:half], im[:half]], 0))
    odd = left_product(tab_ref, 3, cat([re[half:], im[half:]], 0))
    total, diff = even + odd, even - odd
    return cat([total[:half], diff[:half]], 0), cat([total[half:], diff[half:]], 0)


def rolled(value, rows, cols):
    return pltpu.roll(pltpu.roll(value, rows, 0), cols, 1)


MESH = pl.DeviceIdType.MESH
TILE_PARTS = 2
GRAD_PARTS = 4


def kernel(
    pos_ref, cnt_ref, own_ref, probe_ref, amp_ref, tab_ref, ord_ref,
    grad_ref, pgrad_ref,
    tiles, turned, ordered, held, columns, quads, sibs, arrived, pacc, psib, px_buf, py_buf,
    amp_sem, tile_send, tile_recv, pass_send, pass_recv, sib_send, sib_recv, far_send, far_recv,
    out_send, out_recv, ps_send, ps_recv, px_send, px_recv, py_send, py_recv,
    gy_send, gy_recv, gx_send, gx_recv, po_send, po_recv,
):
    slots, size = amp_ref.shape[0], amp_ref.shape[1]
    half = size // 2
    lanes = columns.shape[0]
    tx, ty, pz = lax.axis_index("tx"), lax.axis_index("ty"), lax.axis_index("pz")
    ntx, nty = lax.axis_size("tx"), lax.axis_size("ty")
    other = 1 - pz

    def at(dy, dx):
        return {"ty": lax.rem(ty + dy + nty, nty), "tx": lax.rem(tx + dx + ntx, ntx)}

    def send(src, dst, send_sem, recv_sem, device):
        copy = pltpu.make_async_remote_copy(
            src_ref=src, dst_ref=dst, send_sem=send_sem, recv_sem=recv_sem,
            device_id=device, device_id_type=MESH,
        )
        copy.start()
        return copy

    amp_copies = [
        pltpu.make_async_copy(
            amp_ref.at[:, :, pl.ds(part * 128, 128)], columns.at[part], amp_sem.at[part]
        )
        for part in range(lanes)
    ]
    for copy in amp_copies:
        copy.start()

    partners = [{"pz": other}, at(-1, -1), at(1, 1)]
    partners += [at(0, d) for d in range(1, ntx)] + [at(d, 0) for d in range(1, nty)]
    barrier = pltpu.get_barrier_semaphore()
    for partner in partners:
        pl.semaphore_signal(barrier, inc=1, device_id=partner, device_id_type=MESH)
    pl.semaphore_wait(barrier, len(partners))

    waits = []
    part_rows = size // TILE_PARTS
    tile_copies = []
    for part in range(TILE_PARTS):
        rows = pl.ds(part * part_rows, part_rows)
        for quad, device in enumerate((at(0, -1), at(-1, 0), at(-1, -1))):
            tile_copies.append((quad, part, send(
                own_ref.at[pz, rows], tiles.at[quad, pz, rows],
                tile_send.at[quad, part], tile_recv.at[quad, part], device,
            )))

    row_id = lax.broadcasted_iota(jnp.int32, (size, size), 0)
    col_id = lax.broadcasted_iota(jnp.int32, (size, size), 1)
    row_base, col_base = ty * size, tx * size
    used_count = cnt_ref[0]
    for copy in amp_copies:
        copy.wait()

    def prepare(slot, carry):
        row = pos_ref[slot, 0] - row_base
        col = pos_ref[slot, 1] - col_base
        for p in range(2):
            turned[slot, p] = rolled(probe_ref[p], row, col)
        amp = jnp.concatenate(
            [
                jnp.concatenate(
                    [columns[part, slot, pl.ds(parity, half, 2), :] for part in range(lanes)], 1
                )
                for parity in (0, 1)
            ],
            0,
        )
        high, low = split(amp)
        ordered[slot] = mm(high, ord_ref[...]) + mm(low, ord_ref[...])
        return carry

    lax.fori_loop(0, slots, prepare, 0)
    pacc[...] = jnp.zeros_like(pacc)

    pass_copies = []
    for quad, part, copy in tile_copies:
        copy.wait_recv()
        rows = pl.ds(part * part_rows, part_rows)
        pass_copies.append(send(
            tiles.at[quad, pz, rows], tiles.at[quad, pz, rows],
            pass_send.at[quad, part], pass_recv.at[quad, part], {"pz": other},
        ))
        waits += [copy, pass_copies[-1]]
    for copy in pass_copies:
        copy.wait_recv()

    def visit(slot, carry):
        row = pos_ref[slot, 0] - row_base
        col = pos_ref[slot, 1] - col_base
        used = (slot < used_count).astype(jnp.float32)
        above = row_id < row
        before = col_id < col
        patch = [
            jnp.where(
                above,
                jnp.where(before, tiles[2, p], tiles[1, p]),
                jnp.where(before, tiles[0, p], own_ref[p]),
            )
            for p in range(2)
        ]
        probe = [turned[slot, p] for p in range(2)]
        exit_re = probe[0] * patch[0] - probe[1] * patch[1]
        exit_im = probe[0] * patch[1] + probe[1] * patch[0]
        far_re, far_im = forward(exit_re, exit_im, tab_ref)
        gain = used * (1.0 - ordered[slot] * lax.rsqrt(far_re * far_re + far_im * far_im + 0.01))
        back_re, back_im = backward(far_re * gain, far_im * gain, tab_ref)
        held[slot, 0] = probe[0] * back_re + probe[1] * back_im
        held[slot, 1] = probe[0] * back_im - probe[1] * back_re
        up, left = lax.rem(size - row, size), lax.rem(size - col, size)
        pacc[0] += rolled(patch[0] * back_re + patch[1] * back_im, up, left)
        pacc[1] += rolled(patch[0] * back_im - patch[1] * back_re, up, left)
        return carry

    lax.fori_loop(0, slots, visit, 0)

    probe_copy = send(pacc.at[other], psib, ps_send, ps_recv, {"pz": other})

    chunk = 16
    part_rows = size // GRAD_PARTS
    sib_copies = []
    for part in range(GRAD_PARTS):

        def collect(step, carry):
            base = pl.multiple_of(part * part_rows + step * chunk, chunk)
            row_part = base + lax.broadcasted_iota(jnp.int32, (chunk, size), 0)
            col_part = lax.broadcasted_iota(jnp.int32, (chunk, size), 1)
            for p in range(2):
                sums = [jnp.zeros((chunk, size), jnp.float32) for _ in range(4)]
                for slot in range(slots):
                    above = row_part < pos_ref[slot, 0] - row_base
                    before = col_part < pos_ref[slot, 1] - col_base
                    piece = held[slot, p, pl.ds(base, chunk), :]
                    low = jnp.where(above, piece, 0.0)
                    top = piece - low
                    low_left = jnp.where(before, low, 0.0)
                    top_left = jnp.where(before, top, 0.0)
                    sums = [
                        sums[0] + (top - top_left),
                        sums[1] + top_left,
                        sums[2] + (low - low_left),
                        sums[3] + low_left,
                    ]
                for quad in range(4):
                    quads[quad, p, pl.ds(base, chunk), :] = sums[quad]
            return carry

        lax.fori_loop(0, part_rows // chunk, collect, 0)
        rows = pl.ds(part * part_rows, part_rows)
        sib_copies.append(send(
            quads.at[:, other, rows], sibs.at[:, rows],
            sib_send.at[part], sib_recv.at[part], {"pz": other},
        ))

    far_copies = []
    for part in range(GRAD_PARTS):
        rows = pl.ds(part * part_rows, part_rows)
        sib_copies[part].wait_recv()
        for quad in range(4):
            quads[quad, pz, rows, :] += sibs[quad, rows, :]
        for quad, device in enumerate((at(0, 1), at(1, 0), at(1, 1))):
            far_copies.append(send(
                quads.at[quad + 1, pz, rows], arrived.at[quad, rows],
                far_send.at[quad, part], far_recv.at[quad, part], device,
            ))

    probe_copy.wait_recv()
    pacc[pz] += psib[...]
    base, count = 0, size
    levels = []
    for axis, peers, me, buf, sends, recvs in (
        ("tx", ntx, tx, px_buf, px_send, px_recv), ("ty", nty, ty, py_buf, py_send, py_recv)
    ):
        scatter = count // peers >= 8
        piece = count // peers if scatter else count
        copies = []
        for d in range(1, peers):
            peer = lax.rem(me + d, peers)
            start = pl.multiple_of(base + peer * piece, 8) if scatter else base
            copies.append(send(
                pacc.at[pz, pl.ds(start, piece)], buf.at[d - 1, pl.ds(0, piece)],
                sends.at[d - 1], recvs.at[d - 1], {axis: peer},
            ))
        base = pl.multiple_of(base + me * piece, 8) if scatter else base
        for copy in copies:
            copy.wait()
        total = pacc[pz, pl.ds(base, piece), :]
        for d in range(1, peers):
            total += buf[d - 1, pl.ds(0, piece), :]
        pacc[pz, pl.ds(base, piece), :] = total
        count = piece
        levels.append((axis, peers, me, scatter, base, piece))
    pgrad_ref[pz, pl.ds(base, count), :] = pacc[pz, pl.ds(base, count), :]
    for (axis, peers, me, scatter, base, piece), sends, recvs in zip(
        levels[::-1], (gy_send, gx_send), (gy_recv, gx_recv)
    ):
        if scatter:
            copies = [
                send(
                    pgrad_ref.at[pz, pl.ds(base, piece)], pgrad_ref.at[pz, pl.ds(base, piece)],
                    sends.at[d - 1], recvs.at[d - 1], {axis: lax.rem(me + d, peers)},
                )
                for d in range(1, peers)
            ]
            for copy in copies:
                copy.wait()
    last = send(pgrad_ref.at[pz], pgrad_ref.at[pz], po_send, po_recv, {"pz": other})

    out_copies = []
    for part in range(GRAD_PARTS):
        rows = pl.ds(part * part_rows, part_rows)
        for copy in far_copies[3 * part : 3 * part + 3]:
            copy.wait_recv()
        grad_ref[pz, rows, :] = (
            quads[0, pz, rows, :] + arrived[0, rows, :] + arrived[1, rows, :] + arrived[2, rows, :]
        )
        out_copies.append(send(
            grad_ref.at[pz, rows], grad_ref.at[pz, rows],
            out_send.at[part], out_recv.at[part], {"pz": other},
        ))
    for copy in out_copies + [last]:
        copy.wait()
    for copy in waits + sib_copies + far_copies + [probe_copy]:
        copy.wait_send()


def per_device(object_field, probe_wave, amplitudes, positions, counts):
    size = probe_wave.shape[1]
    slots = positions.shape[0]
    ntx, nty = lax.axis_size("tx"), lax.axis_size("ty")
    vmem = pl.BlockSpec(memory_space=pltpu.VMEM)
    smem = pl.BlockSpec(memory_space=pltpu.SMEM)
    x_piece = size // ntx if size // ntx >= 8 else size
    y_piece = x_piece // nty if x_piece // nty >= 8 else x_piece
    plane = (size, size)
    dma = pltpu.SemaphoreType.DMA

    def buffer(*shape):
        return pltpu.VMEM(shape, jnp.float32)

    lanes = size // 128
    pairs = [(3, TILE_PARTS)] * 2 + [(GRAD_PARTS,), (3, GRAD_PARTS), (GRAD_PARTS,), None]
    pairs += [(ntx - 1,), (nty - 1,), (nty - 1,), (ntx - 1,), None]
    sems = [dma((lanes,))]
    for shape in pairs:
        sems += [dma(shape) if shape else dma] * 2
    return pl.pallas_call(
        kernel,
        out_shape=(
            jax.ShapeDtypeStruct((2,) + plane, jnp.float32),
            jax.ShapeDtypeStruct((2,) + plane, jnp.float32),
        ),
        in_specs=[smem, smem, vmem, vmem, pl.BlockSpec(memory_space=pl.ANY), vmem, vmem],
        out_specs=(vmem, vmem),
        scratch_shapes=[
            buffer(3, 2, *plane),
            buffer(slots, 2, *plane),
            buffer(slots, *plane),
            buffer(slots, 2, *plane),
            buffer(lanes, slots, size, 128),
            buffer(4, 2, *plane),
            buffer(4, *plane),
            buffer(3, *plane),
            buffer(2, *plane),
            buffer(*plane),
            buffer(ntx - 1, x_piece, size),
            buffer(nty - 1, y_piece, size),
        ] + sems,
        compiler_params=pltpu.CompilerParams(
            vmem_limit_bytes=48 * 1024 * 1024, collective_id=0, has_side_effects=True
        ),
    )(
        positions, counts, object_field, probe_wave, amplitudes,
        jnp.asarray(half_tables(size)), jnp.asarray(order_table(size)),
    )


def solution(mesh):
    return jax.shard_map(
        per_device,
        mesh=mesh,
        in_specs=(
            P(None, ("groups", "ty"), "tx"),
            P(),
            P(("groups", "ty", "tx", "pz"), None, None),
            P(("groups", "ty", "tx", "pz"), None),
            P(("groups", "ty", "tx", "pz")),
        ),
        out_specs=(P(None, ("groups", "ty"), "tx"), P("groups", None, None)),
        check_vma=False,
    )
```

```python
import jax
import jax.numpy as jnp
import numpy as np
from jax import lax
from jax.experimental import pallas as pl
from jax.experimental.pallas import tpu as pltpu
from jax.sharding import PartitionSpec as P


def half_tables(size):
    half = size // 2
    pixel = np.arange(half)
    tables = []
    for parity in (0, 1):
        freq = 2 * np.arange(half) + parity
        phase = (freq[:, None] * pixel[None, :] % size) * (2.0 * np.pi / size)
        cos_tab = np.cos(phase) / np.sqrt(size)
        sin_tab = np.sin(phase) / np.sqrt(size)
        full = np.block([[cos_tab, sin_tab], [-sin_tab, cos_tab]])
        tables += [full, full.T]
    full = np.stack(tables)
    high = full.astype(jnp.bfloat16)
    low = (full - high.astype(np.float64)).astype(jnp.bfloat16)
    return np.stack([high, low], axis=1)


def order_table(size):
    order = np.concatenate([np.arange(0, size, 2), np.arange(1, size, 2)])
    table = np.zeros((size, size), np.float32)
    table[order, np.arange(size)] = 1.0
    return table.astype(jnp.bfloat16)


def split(value):
    high = value.astype(jnp.bfloat16)
    low = (value - high.astype(jnp.float32)).astype(jnp.bfloat16)
    return high, low


def mm(left, right):
    return jnp.dot(left, right, preferred_element_type=jnp.float32)


def left_product(tab_ref, which, value):
    high, low = split(value)
    return mm(tab_ref[which, 0], high) + mm(tab_ref[which, 0], low) + mm(tab_ref[which, 1], high)


def right_product(tab_ref, which, value):
    high, low = split(value)
    return mm(high, tab_ref[which, 0]) + mm(low, tab_ref[which, 0]) + mm(high, tab_ref[which, 1])


def forward(re, im, tab_ref):
    half = re.shape[0] // 2
    cat = jnp.concatenate
    even = cat([re[:half] + re[half:], im[:half] + im[half:]], 0)
    odd = cat([re[:half] - re[half:], im[:half] - im[half:]], 0)
    even = left_product(tab_ref, 0, even)
    odd = left_product(tab_ref, 2, odd)
    re = cat([even[:half], odd[:half]], 0)
    im = cat([even[half:], odd[half:]], 0)
    even = cat([re[:, :half] + re[:, half:], im[:, :half] + im[:, half:]], 1)
    odd = cat([re[:, :half] - re[:, half:], im[:, :half] - im[:, half:]], 1)
    even = right_product(tab_ref, 1, even)
    odd = right_product(tab_ref, 3, odd)
    return cat([even[:, :half], odd[:, :half]], 1), cat([even[:, half:], odd[:, half:]], 1)


def backward(re, im, tab_ref):
    half = re.shape[0] // 2
    cat = jnp.concatenate
    even = right_product(tab_ref, 0, cat([re[:, :half], im[:, :half]], 1))
    odd = right_product(tab_ref, 2, cat([re[:, half:], im[:, half:]], 1))
    total, diff = even + odd, even - odd
    re = cat([total[:, :half], diff[:, :half]], 1)
    im = cat([total[:, half:], diff[:, half:]], 1)
    even = left_product(tab_ref, 1, cat([re[:half], im[:half]], 0))
    odd = left_product(tab_ref, 3, cat([re[half:], im[half:]], 0))
    total, diff = even + odd, even - odd
    return cat([total[:half], diff[:half]], 0), cat([total[half:], diff[half:]], 0)


def rolled(value, rows, cols):
    return pltpu.roll(pltpu.roll(value, rows, 0), cols, 1)


MESH = pl.DeviceIdType.MESH
TILE_PARTS = 2
GRAD_PARTS = 4


def kernel(
    pos_ref, cnt_ref, own_hbm, probe_hbm, amp_ref, tab_hbm, ord_hbm,
    grad_ref, pgrad_ref,
    own_ref, probe_ref, tab_ref, ord_ref, tiles, turned, ordered, held, columns, quads, sibs, arrived, pacc, psib, px_buf, py_buf,
    amp_sem, tile_send, tile_recv, pass_send, pass_recv, sib_send, sib_recv, far_send, far_recv,
    out_send, out_recv, ps_send, ps_recv, px_send, px_recv, py_send, py_recv,
    gy_send, gy_recv, gx_send, gx_recv, po_send, po_recv,
):
    slots, size = amp_ref.shape[0], amp_ref.shape[1]
    half = size // 2
    lanes = columns.shape[0]
    tx, ty, pz = lax.axis_index("tx"), lax.axis_index("ty"), lax.axis_index("pz")
    ntx, nty = lax.axis_size("tx"), lax.axis_size("ty")
    other = 1 - pz

    def at(dy, dx):
        return {"ty": lax.rem(ty + dy + nty, nty), "tx": lax.rem(tx + dx + ntx, ntx)}

    def send(src, dst, send_sem, recv_sem, device):
        copy = pltpu.make_async_remote_copy(
            src_ref=src, dst_ref=dst, send_sem=send_sem, recv_sem=recv_sem,
            device_id=device, device_id_type=MESH,
        )
        copy.start()
        return copy

    amp_copies = [
        pltpu.make_async_copy(
            amp_ref.at[:, :, pl.ds(part * 128, 128)], columns.at[part], amp_sem.at[part]
        )
        for part in range(lanes)
    ]
    own_copy, probe_copy, tab_copy, ord_copy = [
        pltpu.make_async_copy(src, dst, amp_sem.at[lanes + i])
        for i, (src, dst) in enumerate(
            ((own_hbm, own_ref), (probe_hbm, probe_ref), (tab_hbm, tab_ref), (ord_hbm, ord_ref))
        )
    ]

    partners = [{"pz": other}]
    partners += [at(0, d) for d in range(1, ntx)] + [at(d, 0) for d in range(1, nty)]
    barrier = pltpu.get_barrier_semaphore()
    for partner in partners:
        pl.semaphore_signal(barrier, inc=1, device_id=partner, device_id_type=MESH)
    for copy in [probe_copy, ord_copy] + amp_copies + [own_copy, tab_copy]:
        copy.start()
    pl.semaphore_wait(barrier, len(partners))

    waits = []
    part_rows = size // TILE_PARTS
    up, left = at(-1, 0), at(0, -1)

    def tile_rows(part):
        return pl.ds(part * part_rows, part_rows)

    def send_tile(src, quad, part, device):
        copy = send(
            src.at[tile_rows(part)], tiles.at[quad, pz, tile_rows(part)],
            tile_send.at[quad, part], tile_recv.at[quad, part], device,
        )
        waits.append(copy)
        return copy

    def pass_on(quad, part):
        copy = send(
            tiles.at[quad, pz, tile_rows(part)], tiles.at[quad, pz, tile_rows(part)],
            pass_send.at[quad, part], pass_recv.at[quad, part], {"pz": other},
        )
        waits.append(copy)
        pass_copies.append(copy)

    first = list(range(TILE_PARTS // 2))
    second = list(range(TILE_PARTS // 2, TILE_PARTS))
    pass_copies = []
    right_copies = {part: send_tile(own_hbm.at[pz], 0, part, left) for part in first + second}
    down_copies = {part: send_tile(own_hbm.at[pz], 1, part, up) for part in second + first}

    row_id = lax.broadcasted_iota(jnp.int32, (size, size), 0)
    col_id = lax.broadcasted_iota(jnp.int32, (size, size), 1)
    row_base, col_base = ty * size, tx * size
    used_count = cnt_ref[0]
    for copy in [probe_copy, ord_copy] + amp_copies:
        copy.wait()

    def prepare(slot, carry):
        row = pos_ref[slot, 0] - row_base
        col = pos_ref[slot, 1] - col_base
        for p in range(2):
            turned[slot, p] = rolled(probe_ref[p], row, col)
        amp = jnp.concatenate(
            [
                jnp.concatenate(
                    [columns[part, slot, pl.ds(parity, half, 2), :] for part in range(lanes)], 1
                )
                for parity in (0, 1)
            ],
            0,
        )
        high, low = split(amp)
        ordered[slot] = mm(high, ord_ref[...]) + mm(low, ord_ref[...])
        return carry

    lax.fori_loop(0, slots, prepare, 0)
    pacc[...] = jnp.zeros_like(pacc)

    diag_copies = {}
    for part_x, part_y in zip(first, second):
        right_copies[part_x].wait_recv()
        diag_copies[part_x] = send_tile(tiles.at[0, pz], 2, part_x, up)
        down_copies[part_y].wait_recv()
        diag_copies[part_y] = send_tile(tiles.at[1, pz], 2, part_y, left)
        pass_on(0, part_x)
        pass_on(1, part_y)
    for part_x, part_y in zip(first, second):
        right_copies[part_y].wait_recv()
        pass_on(0, part_y)
        down_copies[part_x].wait_recv()
        pass_on(1, part_x)
    for part in [part for pair in zip(first, second) for part in pair]:
        diag_copies[part].wait_recv()
        pass_on(2, part)
    own_copy.wait()
    tab_copy.wait()
    for copy in pass_copies:
        copy.wait_recv()

    def visit(slot, carry):
        row = pos_ref[slot, 0] - row_base
        col = pos_ref[slot, 1] - col_base
        used = (slot < used_count).astype(jnp.float32)
        above = row_id < row
        before = col_id < col
        patch = [
            jnp.where(
                above,
                jnp.where(before, tiles[2, p], tiles[1, p]),
                jnp.where(before, tiles[0, p], own_ref[p]),
            )
            for p in range(2)
        ]
        probe = [turned[slot, p] for p in range(2)]
        exit_re = probe[0] * patch[0] - probe[1] * patch[1]
        exit_im = probe[0] * patch[1] + probe[1] * patch[0]
        far_re, far_im = forward(exit_re, exit_im, tab_ref)
        gain = used * (1.0 - ordered[slot] * lax.rsqrt(far_re * far_re + far_im * far_im + 0.01))
        back_re, back_im = backward(far_re * gain, far_im * gain, tab_ref)
        held[slot, 0] = probe[0] * back_re + probe[1] * back_im
        held[slot, 1] = probe[0] * back_im - probe[1] * back_re
        rows_back, cols_back = lax.rem(size - row, size), lax.rem(size - col, size)
        pacc[0] += rolled(patch[0] * back_re + patch[1] * back_im, rows_back, cols_back)
        pacc[1] += rolled(patch[0] * back_im - patch[1] * back_re, rows_back, cols_back)
        return carry

    lax.fori_loop(0, slots, visit, 0, unroll=slots)

    probe_copy = send(pacc.at[other], psib, ps_send, ps_recv, {"pz": other})

    chunk = 16
    part_rows = size // GRAD_PARTS
    sib_copies = {}
    half_parts = GRAD_PARTS // 2
    order = [part + h * half_parts for part in range(half_parts) for h in (0, 1)]
    for part in order:

        def collect(step, carry):
            base = pl.multiple_of(part * part_rows + step * chunk, chunk)
            row_part = base + lax.broadcasted_iota(jnp.int32, (chunk, size), 0)
            col_part = lax.broadcasted_iota(jnp.int32, (chunk, size), 1)
            for p in range(2):
                sums = [jnp.zeros((chunk, size), jnp.float32) for _ in range(4)]
                for slot in range(slots):
                    above = row_part < pos_ref[slot, 0] - row_base
                    before = col_part < pos_ref[slot, 1] - col_base
                    piece = held[slot, p, pl.ds(base, chunk), :]
                    low = jnp.where(above, piece, 0.0)
                    top = piece - low
                    low_left = jnp.where(before, low, 0.0)
                    top_left = jnp.where(before, top, 0.0)
                    sums = [
                        sums[0] + (top - top_left),
                        sums[1] + top_left,
                        sums[2] + (low - low_left),
                        sums[3] + low_left,
                    ]
                for quad in range(4):
                    quads[quad, p, pl.ds(base, chunk), :] = sums[quad]
            return carry

        lax.fori_loop(0, part_rows // chunk, collect, 0)
        rows = pl.ds(part * part_rows, part_rows)
        sib_copies[part] = send(
            quads.at[:, other, rows], sibs.at[:, rows],
            sib_send.at[part], sib_recv.at[part], {"pz": other},
        )

    far_copies = {}

    def send_far(quad, slot, part, device):
        rows = pl.ds(part * part_rows, part_rows)
        far_copies[slot, part] = send(
            quads.at[quad, pz, rows], arrived.at[slot, rows],
            far_send.at[slot, part], far_recv.at[slot, part], device,
        )

    def send_first(part):
        rows = pl.ds(part * part_rows, part_rows)
        sib_copies[part].wait_recv()
        for quad in range(4):
            quads[quad, pz, rows, :] += sibs[quad, rows, :]
        device = at(0, 1) if part < half_parts else at(1, 0)
        send_far(3, 1, part, device)
        send_far(1 if part < half_parts else 2, 0, part, device)

    def send_second(part):
        rows = pl.ds(part * part_rows, part_rows)
        quad = 2 if part < half_parts else 1
        far_copies[1, part].wait_recv()
        quads[quad, pz, rows, :] += arrived[1, rows, :]
        send_far(quad, 2, part, at(1, 0) if part < half_parts else at(0, 1))

    def reduce_start(axis, peers, me, buf, sends, recvs, base, count):
        scatter = count // peers >= 8
        piece = count // peers if scatter else count
        copies = []
        for d in range(1, peers):
            peer = lax.rem(me + d, peers)
            start = pl.multiple_of(base + peer * piece, 8) if scatter else base
            copies.append(send(
                pacc.at[pz, pl.ds(start, piece)], buf.at[d - 1, pl.ds(0, piece)],
                sends.at[d - 1], recvs.at[d - 1], {axis: peer},
            ))
        base = pl.multiple_of(base + me * piece, 8) if scatter else base
        return copies, scatter, base, piece

    def reduce_end(copies, buf, base, piece):
        for copy in copies:
            copy.wait()
        total = pacc[pz, pl.ds(base, piece), :]
        for d in range(len(copies)):
            total += buf[d, pl.ds(0, piece), :]
        pacc[pz, pl.ds(base, piece), :] = total

    def spread_start(axis, peers, me, sends, recvs, scatter, base, piece):
        if not scatter:
            return []
        return [
            send(
                pgrad_ref.at[pz, pl.ds(base, piece)], pgrad_ref.at[pz, pl.ds(base, piece)],
                sends.at[d - 1], recvs.at[d - 1], {axis: lax.rem(me + d, peers)},
            )
            for d in range(1, peers)
        ]

    probe_copy.wait_recv()
    pacc[pz] += psib[...]
    x_copies, x_scatter, x_base, x_piece = reduce_start(
        "tx", ntx, tx, px_buf, px_send, px_recv, 0, size
    )
    for part in order[:2]:
        send_first(part)
    reduce_end(x_copies, px_buf, x_base, x_piece)
    y_copies, y_scatter, y_base, y_piece = reduce_start(
        "ty", nty, ty, py_buf, py_send, py_recv, x_base, x_piece
    )
    for part in order[2:]:
        send_first(part)
    for part in order[:2]:
        send_second(part)
    reduce_end(y_copies, py_buf, y_base, y_piece)
    pgrad_ref[pz, pl.ds(y_base, y_piece), :] = pacc[pz, pl.ds(y_base, y_piece), :]
    copies = spread_start("ty", nty, ty, gy_send, gy_recv, y_scatter, y_base, y_piece)
    for part in order[2:]:
        send_second(part)
    for copy in copies:
        copy.wait()
    copies = spread_start("tx", ntx, tx, gx_send, gx_recv, x_scatter, x_base, x_piece)

    out_copies = []
    for part in order:
        rows = pl.ds(part * part_rows, part_rows)
        far_copies[0, part].wait_recv()
        far_copies[2, part].wait_recv()
        grad_ref[pz, rows, :] = quads[0, pz, rows, :] + arrived[0, rows, :] + arrived[2, rows, :]
        out_copies.append(send(
            grad_ref.at[pz, rows], grad_ref.at[pz, rows],
            out_send.at[part], out_recv.at[part], {"pz": other},
        ))
    for copy in copies:
        copy.wait()
    out_copies.append(
        send(pgrad_ref.at[pz], pgrad_ref.at[pz], po_send, po_recv, {"pz": other})
    )
    for copy in out_copies:
        copy.wait()
    for copy in waits + list(sib_copies.values()) + list(far_copies.values()) + [probe_copy]:
        copy.wait_send()


def per_device(object_field, probe_wave, amplitudes, positions, counts):
    size = probe_wave.shape[1]
    slots = positions.shape[0]
    ntx, nty = lax.axis_size("tx"), lax.axis_size("ty")
    vmem = pl.BlockSpec(memory_space=pltpu.VMEM)
    smem = pl.BlockSpec(memory_space=pltpu.SMEM)
    x_piece = size // ntx if size // ntx >= 8 else size
    y_piece = x_piece // nty if x_piece // nty >= 8 else x_piece
    plane = (size, size)
    dma = pltpu.SemaphoreType.DMA

    def buffer(*shape):
        return pltpu.VMEM(shape, jnp.float32)

    tables, ordering = jnp.asarray(half_tables(size)), jnp.asarray(order_table(size))
    lanes = size // 128
    pairs = [(3, TILE_PARTS)] * 2 + [(GRAD_PARTS,), (3, GRAD_PARTS), (GRAD_PARTS,), None]
    pairs += [(ntx - 1,), (nty - 1,), (nty - 1,), (ntx - 1,), None]
    sems = [dma((lanes + 4,))]
    for shape in pairs:
        sems += [dma(shape) if shape else dma] * 2
    return pl.pallas_call(
        kernel,
        out_shape=(
            jax.ShapeDtypeStruct((2,) + plane, jnp.float32),
            jax.ShapeDtypeStruct((2,) + plane, jnp.float32),
        ),
        in_specs=[smem, smem] + [pl.BlockSpec(memory_space=pl.ANY)] * 5,
        out_specs=(vmem, vmem),
        scratch_shapes=[
            buffer(2, *plane),
            buffer(2, *plane),
            pltpu.VMEM(tables.shape, tables.dtype),
            pltpu.VMEM(ordering.shape, ordering.dtype),
            buffer(3, 2, *plane),
            buffer(slots, 2, *plane),
            buffer(slots, *plane),
            buffer(slots, 2, *plane),
            buffer(lanes, slots, size, 128),
            buffer(4, 2, *plane),
            buffer(4, *plane),
            buffer(3, *plane),
            buffer(2, *plane),
            buffer(*plane),
            buffer(ntx - 1, x_piece, size),
            buffer(nty - 1, y_piece, size),
        ] + sems,
        compiler_params=pltpu.CompilerParams(
            vmem_limit_bytes=48 * 1024 * 1024, collective_id=0, has_side_effects=True
        ),
    )(
        positions, counts, object_field, probe_wave, amplitudes,
        tables, ordering,
    )


def solution(mesh):
    return jax.shard_map(
        per_device,
        mesh=mesh,
        in_specs=(
            P(None, ("groups", "ty"), "tx"),
            P(),
            P(("groups", "ty", "tx", "pz"), None, None),
            P(("groups", "ty", "tx", "pz"), None),
            P(("groups", "ty", "tx", "pz")),
        ),
        out_specs=(P(None, ("groups", "ty"), "tx"), P("groups", None, None)),
        check_vma=False,
    )
```

```python
import jax
import jax.numpy as jnp
import numpy as np
from jax import lax
from jax.experimental import pallas as pl
from jax.experimental.pallas import tpu as pltpu
from jax.sharding import PartitionSpec as P


def half_tables(size):
    half = size // 2
    pixel = np.arange(half)
    tables = []
    for parity in (0, 1):
        freq = 2 * np.arange(half) + parity
        phase = (freq[:, None] * pixel[None, :] % size) * (2.0 * np.pi / size)
        cos_tab = np.cos(phase) / np.sqrt(size)
        sin_tab = np.sin(phase) / np.sqrt(size)
        full = np.block([[cos_tab, sin_tab], [-sin_tab, cos_tab]])
        tables += [full, full.T]
    full = np.stack(tables)
    high = full.astype(jnp.bfloat16)
    low = (full - high.astype(np.float64)).astype(jnp.bfloat16)
    return np.stack([high, low], axis=1)


def order_table(size):
    order = np.concatenate([np.arange(0, size, 2), np.arange(1, size, 2)])
    table = np.zeros((size, size), np.float32)
    table[order, np.arange(size)] = 1.0
    return table.astype(jnp.bfloat16)


def split(value):
    high = value.astype(jnp.bfloat16)
    low = (value - high.astype(jnp.float32)).astype(jnp.bfloat16)
    return high, low


def mm(left, right):
    return jnp.dot(left, right, preferred_element_type=jnp.float32)


def left_product(tab_ref, which, value):
    high, low = split(value)
    return mm(tab_ref[which, 0], high) + mm(tab_ref[which, 0], low) + mm(tab_ref[which, 1], high)


def right_product(tab_ref, which, value):
    high, low = split(value)
    return mm(high, tab_ref[which, 0]) + mm(low, tab_ref[which, 0]) + mm(high, tab_ref[which, 1])


def forward(re, im, tab_ref):
    half = re.shape[0] // 2
    cat = jnp.concatenate
    even = cat([re[:half] + re[half:], im[:half] + im[half:]], 0)
    odd = cat([re[:half] - re[half:], im[:half] - im[half:]], 0)
    even = left_product(tab_ref, 0, even)
    odd = left_product(tab_ref, 2, odd)
    re = cat([even[:half], odd[:half]], 0)
    im = cat([even[half:], odd[half:]], 0)
    even = cat([re[:, :half] + re[:, half:], im[:, :half] + im[:, half:]], 1)
    odd = cat([re[:, :half] - re[:, half:], im[:, :half] - im[:, half:]], 1)
    even = right_product(tab_ref, 1, even)
    odd = right_product(tab_ref, 3, odd)
    return cat([even[:, :half], odd[:, :half]], 1), cat([even[:, half:], odd[:, half:]], 1)


def backward(re, im, tab_ref):
    half = re.shape[0] // 2
    cat = jnp.concatenate
    even = right_product(tab_ref, 0, cat([re[:, :half], im[:, :half]], 1))
    odd = right_product(tab_ref, 2, cat([re[:, half:], im[:, half:]], 1))
    total, diff = even + odd, even - odd
    re = cat([total[:, :half], diff[:, :half]], 1)
    im = cat([total[:, half:], diff[:, half:]], 1)
    even = left_product(tab_ref, 1, cat([re[:half], im[:half]], 0))
    odd = left_product(tab_ref, 3, cat([re[half:], im[half:]], 0))
    total, diff = even + odd, even - odd
    return cat([total[:half], diff[:half]], 0), cat([total[half:], diff[half:]], 0)


def rolled(value, rows, cols):
    return pltpu.roll(pltpu.roll(value, rows, 0), cols, 1)


MESH = pl.DeviceIdType.MESH
TILE_PARTS = 2
GRAD_PARTS = 4


def kernel(
    pos_ref, cnt_ref, own_hbm, probe_hbm, amp_ref, tab_hbm, ord_hbm,
    grad_ref, pgrad_ref,
    own_ref, probe_ref, tab_ref, ord_ref, tiles, turned, ordered, held, columns, quads, sibs, arrived, pacc, psib, px_buf, py_buf,
    amp_sem, tile_send, tile_recv, pass_send, pass_recv, sib_send, sib_recv, far_send, far_recv,
    out_send, out_recv, ps_send, ps_recv, px_send, px_recv, py_send, py_recv,
    gy_send, gy_recv, gx_send, gx_recv, po_send, po_recv,
):
    slots, size = amp_ref.shape[0], amp_ref.shape[1]
    half = size // 2
    lanes = columns.shape[0]
    tx, ty, pz = lax.axis_index("tx"), lax.axis_index("ty"), lax.axis_index("pz")
    ntx, nty = lax.axis_size("tx"), lax.axis_size("ty")
    other = 1 - pz

    def at(dy, dx):
        return {"ty": lax.rem(ty + dy + nty, nty), "tx": lax.rem(tx + dx + ntx, ntx)}

    def send(src, dst, send_sem, recv_sem, device):
        copy = pltpu.make_async_remote_copy(
            src_ref=src, dst_ref=dst, send_sem=send_sem, recv_sem=recv_sem,
            device_id=device, device_id_type=MESH,
        )
        copy.start()
        return copy

    amp_copies = [
        pltpu.make_async_copy(
            amp_ref.at[:, :, pl.ds(part * 128, 128)], columns.at[part], amp_sem.at[part]
        )
        for part in range(lanes)
    ]
    own_copy, probe_copy, tab_copy, ord_copy = [
        pltpu.make_async_copy(src, dst, amp_sem.at[lanes + i])
        for i, (src, dst) in enumerate(
            ((own_hbm, own_ref), (probe_hbm, probe_ref), (tab_hbm, tab_ref), (ord_hbm, ord_ref))
        )
    ]

    partners = [{"pz": other}]
    partners += [at(0, d) for d in range(1, ntx)] + [at(d, 0) for d in range(1, nty)]
    barrier = pltpu.get_barrier_semaphore()
    for partner in partners:
        pl.semaphore_signal(barrier, inc=1, device_id=partner, device_id_type=MESH)
    for copy in [probe_copy, ord_copy] + amp_copies + [own_copy, tab_copy]:
        copy.start()
    pl.semaphore_wait(barrier, len(partners))

    waits = []
    part_rows = size // TILE_PARTS
    up, left = at(-1, 0), at(0, -1)

    def tile_rows(part):
        return pl.ds(part * part_rows, part_rows)

    def send_tile(src, quad, part, device):
        copy = send(
            src.at[tile_rows(part)], tiles.at[quad, pz, tile_rows(part)],
            tile_send.at[quad, part], tile_recv.at[quad, part], device,
        )
        waits.append(copy)
        return copy

    def pass_on(quad, part):
        copy = send(
            tiles.at[quad, pz, tile_rows(part)], tiles.at[quad, pz, tile_rows(part)],
            pass_send.at[quad, part], pass_recv.at[quad, part], {"pz": other},
        )
        waits.append(copy)
        pass_copies.append(copy)

    first = list(range(TILE_PARTS // 2))
    second = list(range(TILE_PARTS // 2, TILE_PARTS))
    pass_copies = []
    right_copies = {part: send_tile(own_hbm.at[pz], 0, part, left) for part in first + second}
    down_copies = {part: send_tile(own_hbm.at[pz], 1, part, up) for part in second + first}

    row_id = lax.broadcasted_iota(jnp.int32, (size, size), 0)
    col_id = lax.broadcasted_iota(jnp.int32, (size, size), 1)
    row_base, col_base = ty * size, tx * size
    used_count = cnt_ref[0]
    for copy in [probe_copy, ord_copy] + amp_copies:
        copy.wait()

    def prepare(slot, carry):
        row = pos_ref[slot, 0] - row_base
        col = pos_ref[slot, 1] - col_base
        for p in range(2):
            turned[slot, p] = rolled(probe_ref[p], row, col)
        amp = jnp.concatenate(
            [
                jnp.concatenate(
                    [columns[part, slot, pl.ds(parity, half, 2), :] for part in range(lanes)], 1
                )
                for parity in (0, 1)
            ],
            0,
        )
        high, low = split(amp)
        ordered[slot] = mm(high, ord_ref[...]) + mm(low, ord_ref[...])
        return carry

    lax.fori_loop(0, slots, prepare, 0)
    pacc[...] = jnp.zeros_like(pacc)

    diag_copies = {}
    for part_x, part_y in zip(first, second):
        right_copies[part_x].wait_recv()
        diag_copies[part_x] = send_tile(tiles.at[0, pz], 2, part_x, up)
        down_copies[part_y].wait_recv()
        diag_copies[part_y] = send_tile(tiles.at[1, pz], 2, part_y, left)
        pass_on(0, part_x)
        pass_on(1, part_y)
    for part_x, part_y in zip(first, second):
        right_copies[part_y].wait_recv()
        pass_on(0, part_y)
        down_copies[part_x].wait_recv()
        pass_on(1, part_x)
    for part in [part for pair in zip(first, second) for part in pair]:
        diag_copies[part].wait_recv()
        pass_on(2, part)
    own_copy.wait()
    tab_copy.wait()
    for copy in pass_copies:
        copy.wait_recv()

    def visit(slot, carry):
        row = pos_ref[slot, 0] - row_base
        col = pos_ref[slot, 1] - col_base
        used = (slot < used_count).astype(jnp.float32)
        above = row_id < row
        before = col_id < col
        patch = [
            jnp.where(
                above,
                jnp.where(before, tiles[2, p], tiles[1, p]),
                jnp.where(before, tiles[0, p], own_ref[p]),
            )
            for p in range(2)
        ]
        probe = [turned[slot, p] for p in range(2)]
        exit_re = probe[0] * patch[0] - probe[1] * patch[1]
        exit_im = probe[0] * patch[1] + probe[1] * patch[0]
        far_re, far_im = forward(exit_re, exit_im, tab_ref)
        gain = used * (1.0 - ordered[slot] * lax.rsqrt(far_re * far_re + far_im * far_im + 0.01))
        back_re, back_im = backward(far_re * gain, far_im * gain, tab_ref)
        held[slot, 0] = probe[0] * back_re + probe[1] * back_im
        held[slot, 1] = probe[0] * back_im - probe[1] * back_re
        rows_back, cols_back = lax.rem(size - row, size), lax.rem(size - col, size)
        pacc[0] += rolled(patch[0] * back_re + patch[1] * back_im, rows_back, cols_back)
        pacc[1] += rolled(patch[0] * back_im - patch[1] * back_re, rows_back, cols_back)
        return carry

    lax.fori_loop(0, slots, visit, 0, unroll=slots)

    probe_copy = send(pacc.at[other], psib, ps_send, ps_recv, {"pz": other})

    chunk = 16
    part_rows = size // GRAD_PARTS
    sib_copies = {}
    half_parts = GRAD_PARTS // 2
    order = [part + h * half_parts for part in range(half_parts) for h in (0, 1)]
    for part in order:

        def collect(step, carry):
            base = pl.multiple_of(part * part_rows + step * chunk, chunk)
            row_part = base + lax.broadcasted_iota(jnp.int32, (chunk, size), 0)
            col_part = lax.broadcasted_iota(jnp.int32, (chunk, size), 1)
            for p in range(2):
                sums = [jnp.zeros((chunk, size), jnp.float32) for _ in range(4)]
                for slot in range(slots):
                    above = row_part < pos_ref[slot, 0] - row_base
                    before = col_part < pos_ref[slot, 1] - col_base
                    piece = held[slot, p, pl.ds(base, chunk), :]
                    low = jnp.where(above, piece, 0.0)
                    top = piece - low
                    low_left = jnp.where(before, low, 0.0)
                    top_left = jnp.where(before, top, 0.0)
                    sums = [
                        sums[0] + (top - top_left),
                        sums[1] + top_left,
                        sums[2] + (low - low_left),
                        sums[3] + low_left,
                    ]
                for quad in range(4):
                    quads[quad, p, pl.ds(base, chunk), :] = sums[quad]
            return carry

        lax.fori_loop(0, part_rows // chunk, collect, 0)
        rows = pl.ds(part * part_rows, part_rows)
        sib_copies[part] = send(
            quads.at[:, other, rows], sibs.at[:, rows],
            sib_send.at[part], sib_recv.at[part], {"pz": other},
        )

    far_copies = {}

    def send_far(quad, slot, part, device):
        rows = pl.ds(part * part_rows, part_rows)
        far_copies[slot, part] = send(
            quads.at[quad, pz, rows], arrived.at[slot, rows],
            far_send.at[slot, part], far_recv.at[slot, part], device,
        )

    def send_first(part):
        rows = pl.ds(part * part_rows, part_rows)
        sib_copies[part].wait_recv()
        for quad in range(4):
            quads[quad, pz, rows, :] += sibs[quad, rows, :]
        device = at(0, 1) if part < half_parts else at(1, 0)
        send_far(3, 1, part, device)
        send_far(1 if part < half_parts else 2, 0, part, device)

    def send_second(part):
        rows = pl.ds(part * part_rows, part_rows)
        quad = 2 if part < half_parts else 1
        far_copies[1, part].wait_recv()
        quads[quad, pz, rows, :] += arrived[1, rows, :]
        send_far(quad, 2, part, at(1, 0) if part < half_parts else at(0, 1))

    def reduce_start(axis, peers, me, buf, sends, recvs, base, count):
        scatter = count // peers >= 8
        piece = count // peers if scatter else count
        copies = []
        for d in range(1, peers):
            peer = lax.rem(me + d, peers)
            start = pl.multiple_of(base + peer * piece, 8) if scatter else base
            copies.append(send(
                pacc.at[pz, pl.ds(start, piece)], buf.at[d - 1, pl.ds(0, piece)],
                sends.at[d - 1], recvs.at[d - 1], {axis: peer},
            ))
        base = pl.multiple_of(base + me * piece, 8) if scatter else base
        return copies, scatter, base, piece

    def reduce_end(copies, buf, base, piece):
        for copy in copies:
            copy.wait()
        total = pacc[pz, pl.ds(base, piece), :]
        for d in range(len(copies)):
            total += buf[d, pl.ds(0, piece), :]
        pacc[pz, pl.ds(base, piece), :] = total

    def spread_start(axis, peers, me, sends, recvs, scatter, base, piece):
        if not scatter:
            return []
        return [
            send(
                pgrad_ref.at[pz, pl.ds(base, piece)], pgrad_ref.at[pz, pl.ds(base, piece)],
                sends.at[d - 1], recvs.at[d - 1], {axis: lax.rem(me + d, peers)},
            )
            for d in range(1, peers)
        ]

    probe_copy.wait_recv()
    pacc[pz] += psib[...]
    x_copies, x_scatter, x_base, x_piece = reduce_start(
        "tx", ntx, tx, px_buf, px_send, px_recv, 0, size
    )
    for part in order[:2]:
        send_first(part)
    reduce_end(x_copies, px_buf, x_base, x_piece)
    y_copies, y_scatter, y_base, y_piece = reduce_start(
        "ty", nty, ty, py_buf, py_send, py_recv, x_base, x_piece
    )
    for part in order[2:]:
        send_first(part)
    for part in order[:2]:
        send_second(part)
    reduce_end(y_copies, py_buf, y_base, y_piece)
    pgrad_ref[pz, pl.ds(y_base, y_piece), :] = pacc[pz, pl.ds(y_base, y_piece), :]
    copies = spread_start("ty", nty, ty, gy_send, gy_recv, y_scatter, y_base, y_piece)
    for part in order[2:]:
        send_second(part)
    for copy in copies:
        copy.wait()
    copies = spread_start("tx", ntx, tx, gx_send, gx_recv, x_scatter, x_base, x_piece)

    out_copies = []
    for part in order:
        rows = pl.ds(part * part_rows, part_rows)
        far_copies[0, part].wait_recv()
        far_copies[2, part].wait_recv()
        grad_ref[pz, rows, :] = quads[0, pz, rows, :] + arrived[0, rows, :] + arrived[2, rows, :]
        out_copies.append(send(
            grad_ref.at[pz, rows], grad_ref.at[pz, rows],
            out_send.at[part], out_recv.at[part], {"pz": other},
        ))
    for copy in copies:
        copy.wait()
    out_copies.append(
        send(pgrad_ref.at[pz], pgrad_ref.at[pz], po_send, po_recv, {"pz": other})
    )
    for copy in out_copies:
        copy.wait()
    for copy in waits + list(sib_copies.values()) + list(far_copies.values()) + [probe_copy]:
        copy.wait_send()


def per_device(object_field, probe_wave, amplitudes, positions, counts):
    size = probe_wave.shape[1]
    slots = positions.shape[0]
    ntx, nty = lax.axis_size("tx"), lax.axis_size("ty")
    vmem = pl.BlockSpec(memory_space=pltpu.VMEM)
    smem = pl.BlockSpec(memory_space=pltpu.SMEM)
    x_piece = size // ntx if size // ntx >= 8 else size
    y_piece = x_piece // nty if x_piece // nty >= 8 else x_piece
    plane = (size, size)
    dma = pltpu.SemaphoreType.DMA

    def buffer(*shape):
        return pltpu.VMEM(shape, jnp.float32)

    tables, ordering = jnp.asarray(half_tables(size)), jnp.asarray(order_table(size))
    lanes = size // 128
    pairs = [(3, TILE_PARTS)] * 2 + [(GRAD_PARTS,), (3, GRAD_PARTS), (GRAD_PARTS,), None]
    pairs += [(ntx - 1,), (nty - 1,), (nty - 1,), (ntx - 1,), None]
    sems = [dma((lanes + 4,))]
    for shape in pairs:
        sems += [dma(shape) if shape else dma] * 2
    return pl.pallas_call(
        kernel,
        out_shape=(
            jax.ShapeDtypeStruct((2,) + plane, jnp.float32),
            jax.ShapeDtypeStruct((2,) + plane, jnp.float32),
        ),
        in_specs=[smem, smem] + [pl.BlockSpec(memory_space=pl.ANY)] * 5,
        out_specs=(vmem, vmem),
        scratch_shapes=[
            buffer(2, *plane),
            buffer(2, *plane),
            pltpu.VMEM(tables.shape, tables.dtype),
            pltpu.VMEM(ordering.shape, ordering.dtype),
            buffer(3, 2, *plane),
            buffer(slots, 2, *plane),
            buffer(slots, *plane),
            buffer(slots, 2, *plane),
            buffer(lanes, slots, size, 128),
            buffer(4, 2, *plane),
            buffer(4, *plane),
            buffer(3, *plane),
            buffer(2, *plane),
            buffer(*plane),
            buffer(ntx - 1, x_piece, size),
            buffer(nty - 1, y_piece, size),
        ] + sems,
        compiler_params=pltpu.CompilerParams(
            vmem_limit_bytes=62 * 1024 * 1024, collective_id=0, has_side_effects=True
        ),
    )(
        positions, counts, object_field, probe_wave, amplitudes,
        tables, ordering,
    )


def solution(mesh):
    return jax.shard_map(
        per_device,
        mesh=mesh,
        in_specs=(
            P(None, ("groups", "ty"), "tx"),
            P(),
            P(("groups", "ty", "tx", "pz"), None, None),
            P(("groups", "ty", "tx", "pz"), None),
            P(("groups", "ty", "tx", "pz")),
        ),
        out_specs=(P(None, ("groups", "ty"), "tx"), P("groups", None, None)),
        check_vma=False,
    )
```
